32 devices in a mesh: orb: 4 (over y, core), grp: 8 (over z, x).
Axes of the slice: x: 2, y: 2, z: 4, core: 2. Of those that a mesh axis runs over, the one named last changes fastest.
Arguments:
- targets: bfloat16 [4, 98304], P('orb'), may hold values from -6 to 6
- partners: bfloat16 [64, 98304], P(('orb', 'grp')), may hold values from -6 to 6
Outputs:
- exchange: float32 [4, 98304], P('orb', 'grp')
The draws below stay inside these ranges and needn't reach their ends.
All inputs are finite; a program needn't handle non-finite values.
Results may differ from the reference program's by a relative error of at most 0.007.
Values may be sent and summed in bfloat16 or wider, within the bound.
A program may use at most 64 MiB of HBM per device.

```python
import math
import jax
import jax.numpy as jnp
from jax import lax

X = 32
Y = 48
Z = 64
TGT = 1
PTN = 2
STEPS = 3
CELLS = 98304
TRIALS = 4
PARTNERS = 64
N_ORB = 4
N_GRP = 8


def raised(values, rng, source, target, parts, factor):
    def block_of(axis_at):
        return (jnp.arange(values.shape[axis_at]) // (values.shape[axis_at] // parts)).reshape((-1,) + (1,) * (values.ndim - 1 - axis_at))

    first = jax.random.permutation(rng, parts)[block_of(target)]
    second = (block_of(target) + parts // 2) % parts
    return jnp.where((block_of(source) == first) | (block_of(source) == second), factor * values, values)


def levels(key, shape, split, low, largest):
    gain, own = 1.0, jax.random.fold_in(key, 6)
    for dim, parts in split:
        steps = jnp.exp(jax.random.uniform(jax.random.fold_in(own, dim), (parts,), jnp.float32, low / len(split), largest / len(split)))
        gain = gain * jnp.repeat(steps, shape[dim] // parts).reshape([-1 if axis == dim else 1 for axis in range(len(shape))])
    return gain


def normal_values(stream_key, shape, width, reach, pieces=(), kind=jnp.bfloat16):
    drawn = jax.random.normal(stream_key, shape, jnp.float32) * width
    if len(pieces) > 0:
        drawn = levels(stream_key, shape, pieces, -0.22, 0.18) * drawn
    return jnp.clip(drawn, min=-reach, max=reach).astype(kind)


def noise_with(stream_key, extent, width, limit, cuts, heavy, kind=jnp.bfloat16):
    array = width * jax.random.normal(stream_key, extent, jnp.float32)
    if cuts:
        array = array * levels(stream_key, extent, cuts, -0.22, 0.18)
    return jnp.clip(raised(array, jax.random.fold_in(stream_key, 3), *heavy), -limit, limit).astype(kind)


def setup_inputs(seed: int = 0) -> dict:
    key_of = jax.random.split(jax.random.key(seed), 3)
    return {
        "targets": normal_values(key_of[0], (TRIALS, CELLS), 1.0, 6.0, ((0, 4),)),
        "partners": noise_with(key_of[1], (PARTNERS, CELLS), 1.0, 6.0, ((0, 32),), (0, 1, 32, 2.75)),
    }


screening = 0.11
spacing = 0.45

def hartley(length):
    indices = jnp.arange(length, dtype=jnp.int32)
    product = indices[:, None] * indices[None, :] % length
    angles = 2.0 * math.pi / length * product.astype(jnp.float32)
    return (jnp.cos(angles) + jnp.sin(angles)).astype(jnp.bfloat16)

def squared_wave(length):
    indices = jnp.arange(length, dtype=jnp.int32)
    folded = jnp.minimum(indices, length - indices).astype(jnp.float32)
    wavenumber = 2.0 * math.pi / (length * spacing) * folded
    return wavenumber * wavenumber

def coulomb_table():
    squares = squared_wave(X)[:, None, None] + squared_wave(Y)[None, :, None] + squared_wave(Z)[None, None, :]
    positive = squares > 0.0
    guarded = jnp.where(positive, squares, 1.0)
    screened = 4.0 * math.pi * (1.0 - jnp.exp(-guarded / (4.0 * screening * screening))) / guarded
    kernel = jnp.where(positive, screened, math.pi / (screening * screening))
    spread = jnp.sqrt(jnp.mean(kernel * kernel))
    return kernel / (spread * (X * Y * Z))

def along(field, table, form):
    return jnp.einsum(form, field.astype(jnp.float32), table.astype(jnp.float32)).astype(jnp.bfloat16)

def pair_terms(target_rows, partner_rows, tables):
    table_x, table_y, table_z, kernel = tables
    target_grid = target_rows.reshape(TGT, 1, X, Y, Z).astype(jnp.float32)
    partner_grid = partner_rows.reshape(1, PTN, X, Y, Z).astype(jnp.float32)
    density = (target_grid * partner_grid).astype(jnp.bfloat16)
    density = along(density, table_z, 'tpxyz,wz->tpxyw')
    density = along(density, table_x, 'tpxyz,wx->tpwyz')
    density = along(density, table_y, 'tpxyz,wy->tpxwz')
    scaled = (density.astype(jnp.float32) * kernel).astype(jnp.bfloat16)
    scaled = along(scaled, table_z, 'tpxyz,wz->tpxyw')
    scaled = along(scaled, table_y, 'tpxyz,wy->tpxwz')
    scaled = along(scaled, table_x, 'tpxyz,wx->tpwyz')
    return lax.optimization_barrier(jnp.sum(scaled.astype(jnp.float32) * partner_grid, axis=1))

def reference(targets, partners):
    tables = (hartley(X), hartley(Y), hartley(Z), coulomb_table())
    cell_count = X * Y * Z
    target_blocks = targets.reshape(N_ORB, TGT, cell_count)
    partner_blocks = partners.reshape(N_ORB, N_GRP, PTN, cell_count)
    factor = 1.0 / math.sqrt(STEPS * N_GRP * PTN)

    def one_block(inputs):
        block_index, target_rows = inputs
        chosen = [lax.dynamic_index_in_dim(partner_blocks, ((block_index - step_index) % N_ORB).astype(jnp.int32), 0, keepdims=False) for step_index in range(STEPS)]
        group_sets = jnp.stack(chosen, axis=1)

        def one_group(running, partner_steps):
            partial_value = jnp.zeros((TGT, X, Y, Z), jnp.float32)
            for step_index in range(STEPS):
                partial_value = partial_value + pair_terms(target_rows, partner_steps[step_index], tables)
            return (running + partial_value, None)
        running, unused = lax.scan(one_group, jnp.zeros((TGT, X, Y, Z), jnp.float32), group_sets)
        return (-running * factor).reshape(TGT, cell_count)
    result = lax.map(one_block, (jnp.arange(N_ORB, dtype=jnp.int32), target_blocks))
    return result.reshape(N_ORB * TGT, cell_count)
```

```python
import functools
import math

import jax
import jax.numpy as jnp
import ml_dtypes
import numpy as np
from jax import lax
from jax.experimental import pallas as pl
from jax.experimental.pallas import tpu as pltpu
from jax.sharding import PartitionSpec as P

X = 32
Y = 48
Z = 64
STEPS = 3
LANES = 128
FOLD = LANES // Z
ROWS_Y = Y // FOLD
EIGHT = 8
GROUPS_Y = ROWS_Y // EIGHT
GROUPS = FOLD * GROUPS_Y
X_BLOCK = 4
X_BLOCKS = X // X_BLOCK
BLOCK_ROWS = X_BLOCK * EIGHT

screening = 0.11
spacing = 0.45
f32 = jnp.float32
bf16 = jnp.bfloat16


def hartley(length):
    indices = np.arange(length)
    angles = 2.0 * math.pi / length * (indices[:, None] * indices[None, :] % length)
    values = (np.cos(angles) + np.sin(angles)).astype(np.float32)
    return values.astype(ml_dtypes.bfloat16).astype(np.float32)


def squared_wave(length):
    indices = np.arange(length)
    folded = np.minimum(indices, length - indices)
    return (2.0 * math.pi / (length * spacing) * folded) ** 2


def coulomb_table():
    squares = (
        squared_wave(X)[:, None, None]
        + squared_wave(Y)[None, :, None]
        + squared_wave(Z)[None, None, :]
    )
    positive = squares > 0.0
    guarded = np.where(positive, squares, 1.0)
    screened = 4.0 * math.pi * (1.0 - np.exp(-guarded / (4.0 * screening * screening))) / guarded
    kernel = np.where(positive, screened, math.pi / (screening * screening))
    spread = np.sqrt(np.mean(kernel * kernel))
    return kernel / (spread * (X * Y * Z))


def tables(copies):
    table_z = np.einsum("zw,ab,pq->pazbqw", hartley(Z), np.eye(FOLD), np.eye(copies))
    table_z = table_z.reshape(copies * LANES, FOLD * copies * Z)
    table_x = np.kron(hartley(X), np.eye(EIGHT))
    h_y = hartley(Y).reshape(GROUPS_Y, EIGHT, FOLD, GROUPS_Y, EIGHT, FOLD)
    table_y = np.einsum("gjahkb,xw->agxjbhwk", h_y, np.eye(X_BLOCK))
    table_y = table_y.reshape(GROUPS * BLOCK_ROWS, GROUPS * BLOCK_ROWS)
    kernel = coulomb_table().reshape(X_BLOCKS, X_BLOCK, GROUPS_Y, EIGHT, FOLD, Z)
    kernel = np.transpose(kernel, (0, 4, 2, 1, 3, 5)).reshape(X_BLOCKS, GROUPS * BLOCK_ROWS, Z)
    kernel = np.tile(kernel, (1, 1, copies))
    narrow = ml_dtypes.bfloat16
    return (
        table_z.astype(narrow),
        np.ascontiguousarray(table_z.T).astype(narrow),
        table_x.astype(narrow),
        table_y.astype(narrow),
        kernel.astype(np.float32),
    )


def body(
    n_orb, n_grp, factor,
    target, own, table_z, table_zt, table_x, table_y, kernel,
    out,
    slots, wide, narrow, total, outbox, inbox,
    send_sems, recv_sems, forward_sems, out_sems, in_sems,
):
    me = lax.axis_index("orb")
    group = lax.axis_index("grp")
    copies = own.shape[0]
    slab = X // n_grp
    slab_rows = slab * ROWS_Y
    padded = outbox.shape[1]

    barrier = pltpu.get_barrier_semaphore()
    orb_steps = sorted({d % n_orb for d in (1, 2, -1, -2)} - {0})
    for distance in orb_steps:
        pl.semaphore_signal(
            barrier, inc=1, device_id=(lax.rem(me + distance, n_orb), group),
            device_id_type=pl.DeviceIdType.MESH,
        )
    for distance in range(1, n_grp):
        pl.semaphore_signal(
            barrier, inc=1, device_id=(me, lax.rem(group + distance, n_grp)),
            device_id_type=pl.DeviceIdType.MESH,
        )
    pl.semaphore_wait(barrier, len(orb_steps) + n_grp - 1)

    def remote(source, slot, p, distance, sems):
        return pltpu.make_async_remote_copy(
            src_ref=source.at[p],
            dst_ref=slots.at[slot, p],
            send_sem=sems.at[p],
            recv_sem=recv_sems.at[slot, p],
            device_id=(lax.rem(me + distance, n_orb), group),
            device_id_type=pl.DeviceIdType.MESH,
        )

    first = [remote(own, 0, p, 1, send_sems.at[0]) for p in range(copies)]
    forward = [remote(slots.at[0], 1, p, 1, forward_sems) for p in range(copies)]
    direct = [remote(own, 1, p, 2, send_sems.at[1]) for p in range(copies)]
    for copy in first:
        copy.start()

    def dot(a, b):
        return jnp.dot(a, b, preferred_element_type=f32)

    def to_spectrum_and_back(partners):
        for at in range(X_BLOCKS):
            rows = slice(at * X_BLOCK * ROWS_Y, (at + 1) * X_BLOCK * ROWS_Y)
            trial = target[rows].astype(f32)
            density = jnp.concatenate(
                [(trial * partners[p, rows].astype(f32)).astype(bf16) for p in range(copies)],
                axis=1,
            )
            wide[at * X_BLOCK : (at + 1) * X_BLOCK] = dot(density, table_z[...]).reshape(
                X_BLOCK, ROWS_Y, FOLD * LANES
            )
        for g in range(GROUPS):
            half, low = g // GROUPS_Y, g % GROUPS_Y * EIGHT
            field = wide[:, low : low + EIGHT, half * LANES : (half + 1) * LANES]
            field = dot(table_x[...], field.reshape(X * EIGHT, LANES).astype(bf16)).astype(bf16)
            narrow[:, g] = field.reshape(X_BLOCKS, BLOCK_ROWS, LANES)
        for at in range(X_BLOCKS):
            field = narrow[at].reshape(GROUPS * BLOCK_ROWS, LANES)
            scaled = (dot(table_y[...], field) * kernel[at]).astype(bf16)
            scaled = dot(table_y[...], scaled).astype(bf16)
            narrow[at] = scaled.reshape(GROUPS, BLOCK_ROWS, LANES)
        for g in range(GROUPS):
            half, low = g // GROUPS_Y, g % GROUPS_Y * EIGHT
            field = dot(table_x[...], narrow[:, g].reshape(X * EIGHT, LANES))
            wide[:, low : low + EIGHT, half * LANES : (half + 1) * LANES] = field.reshape(
                X, EIGHT, LANES
            )

    def terms(partners, first_plane, planes):
        rows = pl.ds(first_plane * ROWS_Y, planes * ROWS_Y)
        field = wide[pl.ds(first_plane, planes)].reshape(planes * ROWS_Y, FOLD * LANES)
        field = dot(field.astype(bf16), table_zt[...])
        result = None
        for p in range(copies):
            term = field[:, p * LANES : (p + 1) * LANES] * partners[p, rows].astype(f32)
            result = term if result is None else result + term
        return result

    to_spectrum_and_back(own)
    for at in range(X_BLOCKS):
        rows = slice(at * X_BLOCK * ROWS_Y, (at + 1) * X_BLOCK * ROWS_Y)
        total[rows] = terms(own, at * X_BLOCK, X_BLOCK)

    for copy in first:
        copy.wait_recv()

    even = lax.rem(me, 2) == 0

    @pl.when(even)
    def _():
        for copy in direct:
            copy.start()
        for copy in forward:
            copy.start()

    to_spectrum_and_back(slots.at[0])
    for at in range(X_BLOCKS):
        rows = slice(at * X_BLOCK * ROWS_Y, (at + 1) * X_BLOCK * ROWS_Y)
        total[rows] += terms(slots.at[0], at * X_BLOCK, X_BLOCK)

    for copy in direct:
        copy.wait_recv()

    to_spectrum_and_back(slots.at[1])

    def summed(owner):
        rows = pl.ds(owner * slab_rows, slab_rows)
        return total[rows] + terms(slots.at[1], owner * slab, slab)

    sent = []
    for distance in range(1, n_grp):
        owner = lax.rem(group + distance, n_grp)
        outbox[distance - 1, 0:slab_rows] = (summed(owner) * factor).astype(bf16)
        if padded > slab_rows:
            outbox[distance - 1, slab_rows:padded] = jnp.zeros((padded - slab_rows, LANES), bf16)
        copy = pltpu.make_async_remote_copy(
            src_ref=outbox.at[distance - 1],
            dst_ref=inbox.at[distance - 1],
            send_sem=out_sems.at[distance - 1],
            recv_sem=in_sems.at[distance - 1],
            device_id=(me, owner),
            device_id_type=pl.DeviceIdType.MESH,
        )
        copy.start()
        sent.append(copy)
    result = summed(group) * factor
    for distance in range(1, n_grp):
        sent[distance - 1].wait_recv()
        result = result + inbox[distance - 1, 0:slab_rows].astype(f32)
    out[...] = result

    for copy in first + sent:
        copy.wait_send()

    @pl.when(even)
    def _():
        for copy in direct + forward:
            copy.wait_send()


def local(n_orb, n_grp, targets, partners):
    copies = partners.shape[0]
    rows = X * ROWS_Y
    slab_rows = rows // n_grp
    padded = -(-slab_rows // 16) * 16
    factor = -1.0 / math.sqrt(STEPS * n_grp * copies)
    constants = tables(copies)
    vmem = pl.BlockSpec(memory_space=pltpu.VMEM)
    result = pl.pallas_call(
        functools.partial(body, n_orb, n_grp, factor),
        out_shape=jax.ShapeDtypeStruct((slab_rows, LANES), f32),
        in_specs=[vmem] * 7,
        out_specs=vmem,
        scratch_shapes=[
            pltpu.VMEM((2, copies, rows, LANES), bf16),
            pltpu.VMEM((X, ROWS_Y, FOLD * LANES), f32),
            pltpu.VMEM((X_BLOCKS, GROUPS, BLOCK_ROWS, LANES), bf16),
            pltpu.VMEM((rows, LANES), f32),
            pltpu.VMEM((n_grp - 1, padded, LANES), bf16),
            pltpu.VMEM((n_grp - 1, padded, LANES), bf16),
            pltpu.SemaphoreType.DMA((2, copies)),
            pltpu.SemaphoreType.DMA((2, copies)),
            pltpu.SemaphoreType.DMA((copies,)),
            pltpu.SemaphoreType.DMA((n_grp - 1,)),
            pltpu.SemaphoreType.DMA((n_grp - 1,)),
        ],
        compiler_params=pltpu.CompilerParams(
            collective_id=0, has_side_effects=True, vmem_limit_bytes=32 * 1024 * 1024
        ),
    )(
        targets.reshape(rows, LANES),
        partners.reshape(copies, rows, LANES),
        *[jnp.asarray(table) for table in constants],
    )
    return result.reshape(1, slab_rows * LANES)


def solution(mesh):
    in_specs = (P("orb", None), P(("orb", "grp"), None))
    out_specs = P("orb", "grp")
    return jax.shard_map(
        functools.partial(local, mesh.shape["orb"], mesh.shape["grp"]),
        mesh=mesh, in_specs=in_specs, out_specs=out_specs, check_vma=False,
    )
```

```python
import functools
import math

import jax
import jax.numpy as jnp
import ml_dtypes
import numpy as np
from jax import lax
from jax.experimental import pallas as pl
from jax.experimental.pallas import tpu as pltpu
from jax.sharding import PartitionSpec as P

X = 32
Y = 48
Z = 64
STEPS = 3
LANES = 128
FOLD = LANES // Z
ROWS_Y = Y // FOLD
EIGHT = 8
GROUPS_Y = ROWS_Y // EIGHT
GROUPS = FOLD * GROUPS_Y
X_BLOCK = 4
X_BLOCKS = X // X_BLOCK
BLOCK_ROWS = X_BLOCK * EIGHT

screening = 0.11
spacing = 0.45
f32 = jnp.float32
bf16 = jnp.bfloat16


def hartley(length):
    indices = np.arange(length)
    angles = 2.0 * math.pi / length * (indices[:, None] * indices[None, :] % length)
    values = (np.cos(angles) + np.sin(angles)).astype(np.float32)
    return values.astype(ml_dtypes.bfloat16).astype(np.float32)


def squared_wave(length):
    indices = np.arange(length)
    folded = np.minimum(indices, length - indices)
    return (2.0 * math.pi / (length * spacing) * folded) ** 2


def coulomb_table():
    squares = (
        squared_wave(X)[:, None, None]
        + squared_wave(Y)[None, :, None]
        + squared_wave(Z)[None, None, :]
    )
    positive = squares > 0.0
    guarded = np.where(positive, squares, 1.0)
    screened = 4.0 * math.pi * (1.0 - np.exp(-guarded / (4.0 * screening * screening))) / guarded
    kernel = np.where(positive, screened, math.pi / (screening * screening))
    spread = np.sqrt(np.mean(kernel * kernel))
    return kernel / (spread * (X * Y * Z))


def tables(copies):
    table_z = np.einsum("zw,ab,pq->pazbqw", hartley(Z), np.eye(FOLD), np.eye(copies))
    table_z = table_z.reshape(copies * LANES, FOLD * copies * Z)
    table_x = np.kron(hartley(X), np.eye(EIGHT))
    h_y = hartley(Y).reshape(GROUPS_Y, EIGHT, FOLD, GROUPS_Y, EIGHT, FOLD)
    table_y = np.einsum("gjahkb,xw->agxjbhwk", h_y, np.eye(X_BLOCK))
    table_y = table_y.reshape(GROUPS * BLOCK_ROWS, GROUPS * BLOCK_ROWS)
    kernel = coulomb_table().reshape(X_BLOCKS, X_BLOCK, GROUPS_Y, EIGHT, FOLD, Z)
    kernel = np.transpose(kernel, (0, 4, 2, 1, 3, 5)).reshape(X_BLOCKS, GROUPS * BLOCK_ROWS, Z)
    kernel = np.tile(kernel, (1, 1, copies))
    narrow = ml_dtypes.bfloat16
    return (
        table_z.astype(narrow),
        np.ascontiguousarray(table_z.T).astype(narrow),
        table_x.astype(narrow),
        table_y.astype(narrow),
        kernel.astype(np.float32),
    )


def body(
    n_orb, n_grp, factor,
    target, own, table_z, table_zt, table_x, table_y, kernel,
    out,
    trials, pool, wide, narrow, total, kept, outbox, inbox, early_outbox, early_inbox, crossing,
    local_sems, first_sems, slot_sems, forward_sems, trial_sems,
    out_sems, in_sems, early_out_sems, early_in_sems, cross_sems,
):
    me = lax.axis_index("orb")
    group = lax.axis_index("grp")
    copies = own.shape[0]
    slab = X // n_grp
    slab_rows = slab * ROWS_Y
    padded = outbox.shape[1]
    odd_index = lax.rem(me, 2)
    even = odd_index == 0

    def block_ahead(distance):
        return (lax.rem(me + distance, n_orb), group)

    own_copy = pltpu.make_async_copy(own, pool.at[0], local_sems.at[0])
    target_copy = pltpu.make_async_copy(target.at[0], trials.at[0], local_sems.at[1])
    own_copy.start()
    target_copy.start()

    barrier = pltpu.get_barrier_semaphore()
    orb_steps = sorted({d % n_orb for d in (1, 2, -1, -2)} - {0})
    for distance in orb_steps:
        pl.semaphore_signal(
            barrier, inc=1, device_id=block_ahead(distance), device_id_type=pl.DeviceIdType.MESH
        )
    for distance in range(1, n_grp):
        pl.semaphore_signal(
            barrier, inc=1, device_id=(me, lax.rem(group + distance, n_grp)),
            device_id_type=pl.DeviceIdType.MESH,
        )
    pl.semaphore_wait(barrier, len(orb_steps) + n_grp - 1)

    def remote(source, destination, send_sem, recv_sem, device):
        return pltpu.make_async_remote_copy(
            src_ref=source, dst_ref=destination, send_sem=send_sem, recv_sem=recv_sem,
            device_id=device, device_id_type=pl.DeviceIdType.MESH,
        )

    trial_copy = remote(
        target.at[0], trials.at[1], trial_sems.at[0], trial_sems.at[1], block_ahead(2)
    )
    first = [
        remote(own.at[p], pool.at[1, p], first_sems.at[p], slot_sems.at[0, p], block_ahead(1))
        for p in range(copies)
    ]
    forward = [
        remote(
            pool.at[1, p], pool.at[2, p], forward_sems.at[p], slot_sems.at[1, p], block_ahead(1)
        )
        for p in range(copies)
    ]
    cross_copy = remote(
        crossing.at[0], crossing.at[1], cross_sems.at[0], cross_sems.at[1], block_ahead(2)
    )

    @pl.when(even)
    def _():
        trial_copy.start()

    for copy in first:
        copy.start()

    def dot(a, b):
        return jnp.dot(a, b, preferred_element_type=f32)

    def to_spectrum_and_back(trial_rows, partners):
        for at in range(X_BLOCKS):
            rows = slice(at * X_BLOCK * ROWS_Y, (at + 1) * X_BLOCK * ROWS_Y)
            trial = trial_rows[rows].astype(f32)
            density = jnp.concatenate(
                [(trial * partners[p, rows].astype(f32)).astype(bf16) for p in range(copies)],
                axis=1,
            )
            wide[at * X_BLOCK : (at + 1) * X_BLOCK] = dot(density, table_z[...]).reshape(
                X_BLOCK, ROWS_Y, FOLD * LANES
            )
        for g in range(GROUPS):
            half, low = g // GROUPS_Y, g % GROUPS_Y * EIGHT
            field = wide[:, low : low + EIGHT, half * LANES : (half + 1) * LANES]
            field = dot(table_x[...], field.reshape(X * EIGHT, LANES).astype(bf16)).astype(bf16)
            narrow[:, g] = field.reshape(X_BLOCKS, BLOCK_ROWS, LANES)
        for at in range(X_BLOCKS):
            field = narrow[at].reshape(GROUPS * BLOCK_ROWS, LANES)
            scaled = (dot(table_y[...], field) * kernel[at]).astype(bf16)
            scaled = dot(table_y[...], scaled).astype(bf16)
            narrow[at] = scaled.reshape(GROUPS, BLOCK_ROWS, LANES)
        for g in range(GROUPS):
            half, low = g // GROUPS_Y, g % GROUPS_Y * EIGHT
            field = dot(table_x[...], narrow[:, g].reshape(X * EIGHT, LANES))
            wide[:, low : low + EIGHT, half * LANES : (half + 1) * LANES] = field.reshape(
                X, EIGHT, LANES
            )

    def terms(partners, first_plane, planes):
        rows = pl.ds(first_plane * ROWS_Y, planes * ROWS_Y)
        field = wide[pl.ds(first_plane, planes)].reshape(planes * ROWS_Y, FOLD * LANES)
        field = dot(field.astype(bf16), table_zt[...])
        result = None
        for p in range(copies):
            term = field[:, p * LANES : (p + 1) * LANES] * partners[p, rows].astype(f32)
            result = term if result is None else result + term
        return result

    def put(place, value):
        place[0:slab_rows] = value.astype(bf16)
        if padded > slab_rows:
            place[slab_rows:padded] = jnp.zeros((padded - slab_rows, LANES), bf16)

    def to_owner(source, destination, sends, arrivals, distance):
        return remote(
            source.at[distance - 1], destination.at[distance - 1],
            sends.at[distance - 1], arrivals.at[distance - 1],
            (me, lax.rem(group + distance, n_grp)),
        )

    early = [
        to_owner(early_outbox, early_inbox, early_out_sems, early_in_sems, distance)
        for distance in range(1, n_grp)
    ]
    late = [
        to_owner(outbox, inbox, out_sems, in_sems, distance) for distance in range(1, n_grp)
    ]

    to_spectrum_and_back(target.at[0], own)
    for at in range(X_BLOCKS):
        rows = slice(at * X_BLOCK * ROWS_Y, (at + 1) * X_BLOCK * ROWS_Y)
        total[rows] = terms(own, at * X_BLOCK, X_BLOCK)

    own_copy.wait()
    target_copy.wait()

    @pl.when(even)
    def _():
        trial_copy.wait_recv()

    @pl.when(jnp.logical_not(even))
    def _():
        for copy in first:
            copy.wait_recv()

    middle = pool.at[odd_index]
    to_spectrum_and_back(trials.at[1 - odd_index], middle)

    @pl.when(even)
    def _():
        for distance in range(1, n_grp):
            owner = lax.rem(group + distance, n_grp)
            put(early_outbox.at[distance - 1], terms(middle, owner * slab, slab) * factor)
            early[distance - 1].start()
        kept[...] = terms(middle, group * slab, slab) * factor
        for copy in first:
            copy.wait_recv()
        for copy in forward:
            copy.start()

    @pl.when(jnp.logical_not(even))
    def _():
        for at in range(X_BLOCKS):
            rows = slice(at * X_BLOCK * ROWS_Y, (at + 1) * X_BLOCK * ROWS_Y)
            total[rows] += terms(middle, at * X_BLOCK, X_BLOCK)
        for copy in forward:
            copy.wait_recv()

    last = pool.at[1 + odd_index]
    to_spectrum_and_back(target.at[0], last)

    def summed(owner):
        rows = pl.ds(owner * slab_rows, slab_rows)
        return (total[rows] + terms(last, owner * slab, slab)) * factor

    for distance in range(1, n_grp):
        put(outbox.at[distance - 1], summed(lax.rem(group + distance, n_grp)))
        late[distance - 1].start()
    out[...] = summed(group)

    @pl.when(even)
    def _():
        crossed = kept[...]
        for distance in range(1, n_grp):
            early[distance - 1].wait_recv()
            crossed = crossed + early_inbox[distance - 1, 0:slab_rows].astype(f32)
        put(crossing.at[0], crossed)
        cross_copy.start()

    result = out[...]
    for distance in range(1, n_grp):
        late[distance - 1].wait_recv()
        result = result + inbox[distance - 1, 0:slab_rows].astype(f32)
    out[...] = result

    for copy in first + late:
        copy.wait_send()

    @pl.when(even)
    def _():
        cross_copy.wait_recv()
        out[...] += crossing[1, 0:slab_rows].astype(f32)
        for copy in forward + early + [trial_copy, cross_copy]:
            copy.wait_send()


def local(n_orb, n_grp, targets, partners):
    copies = partners.shape[0]
    rows = X * ROWS_Y
    slab_rows = rows // n_grp
    padded = -(-slab_rows // 16) * 16
    factor = -1.0 / math.sqrt(STEPS * n_grp * copies)
    constants = tables(copies)
    vmem = pl.BlockSpec(memory_space=pltpu.VMEM)
    box = pltpu.VMEM((n_grp - 1, padded, LANES), bf16)
    dma = pltpu.SemaphoreType.DMA
    result = pl.pallas_call(
        functools.partial(body, n_orb, n_grp, factor),
        out_shape=jax.ShapeDtypeStruct((slab_rows, LANES), f32),
        in_specs=[vmem] * 7,
        out_specs=vmem,
        scratch_shapes=[
            pltpu.VMEM((2, rows, LANES), bf16),
            pltpu.VMEM((3, copies, rows, LANES), bf16),
            pltpu.VMEM((X, ROWS_Y, FOLD * LANES), f32),
            pltpu.VMEM((X_BLOCKS, GROUPS, BLOCK_ROWS, LANES), bf16),
            pltpu.VMEM((rows, LANES), f32),
            pltpu.VMEM((slab_rows, LANES), f32),
            box, box, box, box,
            pltpu.VMEM((2, padded, LANES), bf16),
            dma((2,)), dma((copies,)), dma((2, copies)), dma((copies,)), dma((2,)),
            dma((n_grp - 1,)), dma((n_grp - 1,)), dma((n_grp - 1,)), dma((n_grp - 1,)), dma((2,)),
        ],
        compiler_params=pltpu.CompilerParams(
            collective_id=0, has_side_effects=True, vmem_limit_bytes=32 * 1024 * 1024
        ),
    )(
        targets.reshape(1, rows, LANES),
        partners.reshape(copies, rows, LANES),
        *[jnp.asarray(table) for table in constants],
    )
    return result.reshape(1, slab_rows * LANES)


def solution(mesh):
    in_specs = (P("orb", None), P(("orb", "grp"), None))
    out_specs = P("orb", "grp")
    return jax.shard_map(
        functools.partial(local, mesh.shape["orb"], mesh.shape["grp"]),
        mesh=mesh, in_specs=in_specs, out_specs=out_specs, check_vma=False,
    )
```

```python
import functools
import math

import jax
import jax.numpy as jnp
import ml_dtypes
import numpy as np
from jax import lax
from jax.experimental import pallas as pl
from jax.experimental.pallas import tpu as pltpu
from jax.sharding import PartitionSpec as P

X = 32
Y = 48
Z = 64
STEPS = 3
LANES = 128
FOLD = LANES // Z
ROWS_Y = Y // FOLD
EIGHT = 8
GROUPS_Y = ROWS_Y // EIGHT
GROUPS = FOLD * GROUPS_Y
X_BLOCK = 4
X_BLOCKS = X // X_BLOCK
BLOCK_ROWS = X_BLOCK * EIGHT

screening = 0.11
spacing = 0.45
f32 = jnp.float32
bf16 = jnp.bfloat16


def hartley(length):
    indices = np.arange(length)
    angles = 2.0 * math.pi / length * (indices[:, None] * indices[None, :] % length)
    values = (np.cos(angles) + np.sin(angles)).astype(np.float32)
    return values.astype(ml_dtypes.bfloat16).astype(np.float32)


def squared_wave(length):
    indices = np.arange(length)
    folded = np.minimum(indices, length - indices)
    return (2.0 * math.pi / (length * spacing) * folded) ** 2


def coulomb_table():
    squares = (
        squared_wave(X)[:, None, None]
        + squared_wave(Y)[None, :, None]
        + squared_wave(Z)[None, None, :]
    )
    positive = squares > 0.0
    guarded = np.where(positive, squares, 1.0)
    screened = 4.0 * math.pi * (1.0 - np.exp(-guarded / (4.0 * screening * screening))) / guarded
    kernel = np.where(positive, screened, math.pi / (screening * screening))
    spread = np.sqrt(np.mean(kernel * kernel))
    return kernel / (spread * (X * Y * Z))


def tables(copies):
    table_z = np.einsum("zw,ab,pq->pazbqw", hartley(Z), np.eye(FOLD), np.eye(copies))
    table_z = table_z.reshape(copies * LANES, FOLD * copies * Z)
    table_x = np.kron(hartley(X), np.eye(EIGHT))
    h_y = hartley(Y).reshape(GROUPS_Y, EIGHT, FOLD, GROUPS_Y, EIGHT, FOLD)
    table_y = np.einsum("gjahkb,xw->agxjbhwk", h_y, np.eye(X_BLOCK))
    table_y = table_y.reshape(GROUPS * BLOCK_ROWS, GROUPS * BLOCK_ROWS)
    kernel = coulomb_table().reshape(X_BLOCKS, X_BLOCK, GROUPS_Y, EIGHT, FOLD, Z)
    kernel = np.transpose(kernel, (0, 4, 2, 1, 3, 5)).reshape(X_BLOCKS, GROUPS * BLOCK_ROWS, Z)
    kernel = np.tile(kernel, (1, 1, copies))
    narrow = ml_dtypes.bfloat16
    return (
        table_z.astype(narrow),
        np.ascontiguousarray(table_z.T).astype(narrow),
        table_x.astype(narrow),
        table_y.astype(narrow),
        kernel.astype(np.float32),
    )


def body(
    n_orb, n_grp, factor,
    target, own, table_z, table_zt, table_x, table_y, kernel,
    out,
    trials, pool, wide, narrow, total, outbox, inbox, far_outbox, far_inbox,
    local_sem, swap_sems, trial_sems, out_sems, in_sems, far_out_sems, far_in_sems,
):
    me = lax.axis_index("orb")
    group = lax.axis_index("grp")
    copies = own.shape[0]
    slab = X // n_grp
    slab_rows = slab * ROWS_Y
    padded = outbox.shape[1]
    odd_index = lax.rem(me, 2)
    even = odd_index == 0

    sibling = (me + 1 - 2 * odd_index, group)
    ahead = lax.rem(me + 2, n_orb)
    behind = lax.rem(me + n_orb - 2, n_orb)

    own_copy = pltpu.make_async_copy(own, pool.at[0], local_sem)
    own_copy.start()

    barrier = pltpu.get_barrier_semaphore()
    met = [sibling]
    for distance in range(n_grp):
        other = lax.rem(group + distance, n_grp)
        met += [(me, other)] * (distance > 0) + [(ahead, other)] + [(behind, other)] * (n_orb > 4)
    for device in met:
        pl.semaphore_signal(
            barrier, inc=1, device_id=device, device_id_type=pl.DeviceIdType.MESH
        )
    trials[0] = target[...].astype(bf16)
    pl.semaphore_wait(barrier, len(met))

    def remote(source, destination, send_sem, recv_sem, device):
        return pltpu.make_async_remote_copy(
            src_ref=source, dst_ref=destination, send_sem=send_sem, recv_sem=recv_sem,
            device_id=device, device_id_type=pl.DeviceIdType.MESH,
        )

    trial_copy = remote(
        trials.at[0], trials.at[1], trial_sems.at[0], trial_sems.at[1], (behind, group)
    )
    swap = [
        remote(own.at[p], pool.at[1, p], swap_sems.at[0, p], swap_sems.at[1, p], sibling)
        for p in range(copies)
    ]

    trial_copy.start()

    for copy in swap:
        copy.start()

    def dot(a, b):
        return jnp.dot(a, b, preferred_element_type=f32)

    def to_spectrum_and_back(trial_rows, partners):
        for at in range(X_BLOCKS):
            rows = slice(at * X_BLOCK * ROWS_Y, (at + 1) * X_BLOCK * ROWS_Y)
            trial = trial_rows[rows].astype(f32)
            density = jnp.concatenate(
                [(trial * partners[p, rows].astype(f32)).astype(bf16) for p in range(copies)],
                axis=1,
            )
            wide[at * X_BLOCK : (at + 1) * X_BLOCK] = dot(density, table_z[...]).reshape(
                X_BLOCK, ROWS_Y, FOLD * LANES
            )
        for g in range(GROUPS):
            half, low = g // GROUPS_Y, g % GROUPS_Y * EIGHT
            field = wide[:, low : low + EIGHT, half * LANES : (half + 1) * LANES]
            field = dot(table_x[...], field.reshape(X * EIGHT, LANES).astype(bf16)).astype(bf16)
            narrow[:, g] = field.reshape(X_BLOCKS, BLOCK_ROWS, LANES)
        for at in range(X_BLOCKS):
            field = narrow[at].reshape(GROUPS * BLOCK_ROWS, LANES)
            scaled = (dot(table_y[...], field) * kernel[at]).astype(bf16)
            scaled = dot(table_y[...], scaled).astype(bf16)
            narrow[at] = scaled.reshape(GROUPS, BLOCK_ROWS, LANES)
        for g in range(GROUPS):
            half, low = g // GROUPS_Y, g % GROUPS_Y * EIGHT
            field = dot(table_x[...], narrow[:, g].reshape(X * EIGHT, LANES))
            wide[:, low : low + EIGHT, half * LANES : (half + 1) * LANES] = field.reshape(
                X, EIGHT, LANES
            )

    def terms(partners, first_plane, planes):
        rows = pl.ds(first_plane * ROWS_Y, planes * ROWS_Y)
        field = wide[pl.ds(first_plane, planes)].reshape(planes * ROWS_Y, FOLD * LANES)
        field = dot(field.astype(bf16), table_zt[...])
        result = None
        for p in range(copies):
            term = field[:, p * LANES : (p + 1) * LANES] * partners[p, rows].astype(f32)
            result = term if result is None else result + term
        return result

    def put(place, value):
        place[0:slab_rows] = value.astype(bf16)
        if padded > slab_rows:
            place[slab_rows:padded] = jnp.zeros((padded - slab_rows, LANES), bf16)

    def to_owner(source, destination, sends, arrivals, orb, distance):
        return remote(
            source.at[distance], destination.at[distance], sends.at[distance],
            arrivals.at[distance], (orb, lax.rem(group + distance, n_grp)),
        )

    near = [
        to_owner(outbox, inbox, out_sems, in_sems, me, distance) for distance in range(1, n_grp)
    ]
    far = [
        to_owner(far_outbox, far_inbox, far_out_sems, far_in_sems, ahead, distance)
        for distance in range(n_grp)
    ]

    def store_total(partners):
        for at in range(X_BLOCKS):
            rows = slice(at * X_BLOCK * ROWS_Y, (at + 1) * X_BLOCK * ROWS_Y)
            total[rows] = terms(partners, at * X_BLOCK, X_BLOCK)

    def send_out(partners, add_total, box, sends, mine):
        def summed(owner):
            value = terms(partners, owner * slab, slab)
            if add_total:
                value = value + total[pl.ds(owner * slab_rows, slab_rows)]
            return value * factor

        for distance in range(1, n_grp):
            put(box.at[distance], summed(lax.rem(group + distance, n_grp)))
            sends[distance - n_grp].start()
        if mine is None:
            put(box.at[0], summed(group))
            sends[0].start()
        else:
            mine[...] = summed(group)

    to_spectrum_and_back(trials.at[0], own)

    @pl.when(even)
    def _():
        send_out(own, False, outbox, near, out)

    @pl.when(jnp.logical_not(even))
    def _():
        store_total(own)

    own_copy.wait()

    @pl.when(even)
    def _():
        trial_copy.wait_recv()

    @pl.when(jnp.logical_not(even))
    def _():
        for copy in swap:
            copy.wait_recv()

    middle = pool.at[odd_index]
    to_spectrum_and_back(trials.at[1 - odd_index], middle)

    @pl.when(even)
    def _():
        store_total(middle)
        for copy in swap:
            copy.wait_recv()

    @pl.when(jnp.logical_not(even))
    def _():
        send_out(middle, True, outbox, near, out)
        total[...] = jnp.zeros_like(total)
        trial_copy.wait_recv()

    last = pool.at[1 - odd_index]
    to_spectrum_and_back(trials.at[1], last)
    send_out(last, True, far_outbox, far, None)

    result = out[...]
    for distance in range(1, n_grp):
        near[distance - 1].wait_recv()
        result = result + inbox[distance, 0:slab_rows].astype(f32)
    for distance in range(n_grp):
        far[distance].wait_recv()
        result = result + far_inbox[distance, 0:slab_rows].astype(f32)
    out[...] = result
    for copy in swap + near + far + [trial_copy]:
        copy.wait_send()


def local(n_orb, n_grp, targets, partners):
    copies = partners.shape[0]
    rows = X * ROWS_Y
    slab_rows = rows // n_grp
    padded = -(-slab_rows // 16) * 16
    factor = -1.0 / math.sqrt(STEPS * n_grp * copies)
    constants = tables(copies)
    vmem = pl.BlockSpec(memory_space=pltpu.VMEM)
    box = pltpu.VMEM((n_grp, padded, LANES), bf16)
    dma = pltpu.SemaphoreType.DMA
    result = pl.pallas_call(
        functools.partial(body, n_orb, n_grp, factor),
        out_shape=jax.ShapeDtypeStruct((slab_rows, LANES), f32),
        in_specs=[vmem] * 7,
        out_specs=vmem,
        scratch_shapes=[
            pltpu.VMEM((2, rows, LANES), bf16),
            pltpu.VMEM((3, copies, rows, LANES), bf16),
            pltpu.VMEM((X, ROWS_Y, FOLD * LANES), f32),
            pltpu.VMEM((X_BLOCKS, GROUPS, BLOCK_ROWS, LANES), bf16),
            pltpu.VMEM((rows, LANES), f32),
            box, box, box, box,
            dma, dma((2, copies)), dma((2,)),
            dma((n_grp,)), dma((n_grp,)), dma((n_grp,)), dma((n_grp,)),
        ],
        compiler_params=pltpu.CompilerParams(
            collective_id=0, has_side_effects=True, vmem_limit_bytes=32 * 1024 * 1024
        ),
    )(
        lax.optimization_barrier(targets.astype(f32)).reshape(rows, LANES),
        partners.reshape(copies, rows, LANES),
        *[jnp.asarray(table) for table in constants],
    )
    return result.reshape(1, slab_rows * LANES)


def solution(mesh):
    in_specs = (P("orb", None), P(("orb", "grp"), None))
    out_specs = P("orb", "grp")
    return jax.shard_map(
        functools.partial(local, mesh.shape["orb"], mesh.shape["grp"]),
        mesh=mesh, in_specs=in_specs, out_specs=out_specs, check_vma=False,
    )
```

```python
import functools
import math

import jax
import jax.numpy as jnp
import ml_dtypes
import numpy as np
from jax import lax
from jax.experimental import pallas as pl
from jax.experimental.pallas import tpu as pltpu
from jax.sharding import PartitionSpec as P

X = 32
Y = 48
Z = 64
STEPS = 3
LANES = 128
FOLD = LANES // Z
ROWS_Y = Y // FOLD
EIGHT = 8
GROUPS_Y = ROWS_Y // EIGHT
GROUPS = FOLD * GROUPS_Y
X_BLOCK = 4
X_BLOCKS = X // X_BLOCK
BLOCK_ROWS = X_BLOCK * EIGHT

screening = 0.11
spacing = 0.45
f32 = jnp.float32
bf16 = jnp.bfloat16


def hartley(length):
    indices = np.arange(length)
    angles = 2.0 * math.pi / length * (indices[:, None] * indices[None, :] % length)
    values = (np.cos(angles) + np.sin(angles)).astype(np.float32)
    return values.astype(ml_dtypes.bfloat16).astype(np.float32)


def squared_wave(length):
    indices = np.arange(length)
    folded = np.minimum(indices, length - indices)
    return (2.0 * math.pi / (length * spacing) * folded) ** 2


def coulomb_table():
    squares = (
        squared_wave(X)[:, None, None]
        + squared_wave(Y)[None, :, None]
        + squared_wave(Z)[None, None, :]
    )
    positive = squares > 0.0
    guarded = np.where(positive, squares, 1.0)
    screened = 4.0 * math.pi * (1.0 - np.exp(-guarded / (4.0 * screening * screening))) / guarded
    kernel = np.where(positive, screened, math.pi / (screening * screening))
    spread = np.sqrt(np.mean(kernel * kernel))
    return kernel / (spread * (X * Y * Z))


def tables(copies):
    table_z = np.einsum("zw,ab,pq->pazbqw", hartley(Z), np.eye(FOLD), np.eye(copies))
    table_z = table_z.reshape(copies * LANES, FOLD * copies * Z)
    table_x = np.kron(hartley(X), np.eye(EIGHT))
    h_y = hartley(Y).reshape(GROUPS_Y, EIGHT, FOLD, GROUPS_Y, EIGHT, FOLD)
    table_y = np.einsum("gjahkb,xw->agxjbhwk", h_y, np.eye(X_BLOCK))
    table_y = table_y.reshape(GROUPS * BLOCK_ROWS, GROUPS * BLOCK_ROWS)
    kernel = coulomb_table().reshape(X_BLOCKS, X_BLOCK, GROUPS_Y, EIGHT, FOLD, Z)
    kernel = np.transpose(kernel, (0, 4, 2, 1, 3, 5)).reshape(X_BLOCKS, GROUPS * BLOCK_ROWS, Z)
    kernel = np.tile(kernel, (1, 1, copies))
    narrow = ml_dtypes.bfloat16
    return (
        table_z.astype(narrow),
        np.ascontiguousarray(table_z.T).astype(narrow),
        table_x.astype(narrow),
        table_y.astype(narrow),
        kernel.astype(np.float32),
    )


def body(
    n_orb, n_grp, factor,
    target, own, table_z, table_zt, table_x, table_y, kernel,
    out,
    trials, pool, wide, narrow, total, outbox, inbox, far_outbox, far_inbox,
    local_sem, swap_sems, trial_sems, out_sems, in_sems, far_out_sems, far_in_sems,
):
    me = lax.axis_index("orb")
    group = lax.axis_index("grp")
    copies = own.shape[0]
    slab = X // n_grp
    slab_rows = slab * ROWS_Y
    padded = outbox.shape[1]
    odd_index = lax.rem(me, 2)
    even = odd_index == 0

    sibling = (me + 1 - 2 * odd_index, group)
    ahead = lax.rem(me + 2, n_orb)
    behind = lax.rem(me + n_orb - 2, n_orb)

    own_copy = pltpu.make_async_copy(own, pool.at[0], local_sem)
    own_copy.start()

    barrier = pltpu.get_barrier_semaphore()
    met = [sibling]
    for distance in range(n_grp):
        other = lax.rem(group + distance, n_grp)
        met += [(me, other)] * (distance > 0) + [(ahead, other)] + [(behind, other)] * (n_orb > 4)
    for device in met:
        pl.semaphore_signal(
            barrier, inc=1, device_id=device, device_id_type=pl.DeviceIdType.MESH
        )
    trials[0] = target[...].astype(bf16)
    pl.semaphore_wait(barrier, len(met))

    def remote(source, destination, send_sem, recv_sem, device):
        return pltpu.make_async_remote_copy(
            src_ref=source, dst_ref=destination, send_sem=send_sem, recv_sem=recv_sem,
            device_id=device, device_id_type=pl.DeviceIdType.MESH,
        )

    trial_copy = remote(
        trials.at[0], trials.at[1], trial_sems.at[0], trial_sems.at[1], (behind, group)
    )
    swap = [
        remote(own.at[p], pool.at[1, p], swap_sems.at[0, p], swap_sems.at[1, p], sibling)
        for p in range(copies)
    ]

    trial_copy.start()

    for copy in swap:
        copy.start()

    def dot(a, b):
        return jnp.dot(a, b, preferred_element_type=f32)

    def to_spectrum_and_back(trial_rows, partners):
        for at in range(X_BLOCKS):
            rows = slice(at * X_BLOCK * ROWS_Y, (at + 1) * X_BLOCK * ROWS_Y)
            trial = trial_rows[rows]
            density = jnp.concatenate(
                [trial * partners[p, rows] for p in range(copies)],
                axis=1,
            )
            wide[at * X_BLOCK : (at + 1) * X_BLOCK] = dot(density, table_z[...]).reshape(
                X_BLOCK, ROWS_Y, FOLD * LANES
            )
        for g in range(GROUPS_Y):
            low = g * EIGHT
            field = wide[:, low : low + EIGHT].reshape(X * EIGHT, FOLD * LANES).astype(bf16)
            field = dot(table_x[...], field).astype(bf16)
            for half in range(FOLD):
                narrow[:, half * GROUPS_Y + g] = field[
                    :, half * LANES : (half + 1) * LANES
                ].reshape(X_BLOCKS, BLOCK_ROWS, LANES)
        for at in range(0, X_BLOCKS, 2):
            two = (at, at + 1)
            field = jnp.concatenate(
                [narrow[b].reshape(GROUPS * BLOCK_ROWS, LANES) for b in two], axis=1
            )
            table = jnp.concatenate([kernel[b] for b in two], axis=1)
            scaled = (dot(table_y[...], field) * table).astype(bf16)
            scaled = dot(table_y[...], scaled).astype(bf16)
            for i, b in enumerate(two):
                narrow[b] = scaled[:, i * LANES : (i + 1) * LANES].reshape(
                    GROUPS, BLOCK_ROWS, LANES
                )
        for g in range(GROUPS_Y):
            low = g * EIGHT
            field = jnp.concatenate(
                [
                    narrow[:, half * GROUPS_Y + g].reshape(X * EIGHT, LANES)
                    for half in range(FOLD)
                ],
                axis=1,
            )
            wide[:, low : low + EIGHT] = dot(table_x[...], field).reshape(
                X, EIGHT, FOLD * LANES
            )

    def terms(partners, first_plane, planes):
        rows = pl.ds(first_plane * ROWS_Y, planes * ROWS_Y)
        field = wide[pl.ds(first_plane, planes)].reshape(planes * ROWS_Y, FOLD * LANES)
        field = dot(field.astype(bf16), table_zt[...])
        result = None
        for p in range(copies):
            term = field[:, p * LANES : (p + 1) * LANES] * partners[p, rows].astype(f32)
            result = term if result is None else result + term
        return result

    def put(place, value):
        place[0:slab_rows] = value.astype(bf16)
        if padded > slab_rows:
            place[slab_rows:padded] = jnp.zeros((padded - slab_rows, LANES), bf16)

    def to_owner(source, destination, sends, arrivals, orb, distance):
        return remote(
            source.at[distance], destination.at[distance], sends.at[distance],
            arrivals.at[distance], (orb, lax.rem(group + distance, n_grp)),
        )

    near = [
        to_owner(outbox, inbox, out_sems, in_sems, me, distance) for distance in range(1, n_grp)
    ]
    far = [
        to_owner(far_outbox, far_inbox, far_out_sems, far_in_sems, ahead, distance)
        for distance in range(n_grp)
    ]

    def store_total(partners):
        for at in range(X_BLOCKS):
            rows = slice(at * X_BLOCK * ROWS_Y, (at + 1) * X_BLOCK * ROWS_Y)
            total[rows] = terms(partners, at * X_BLOCK, X_BLOCK)

    def send_out(partners, add_total, box, sends, mine):
        def summed(owner):
            value = terms(partners, owner * slab, slab)
            if add_total:
                value = value + total[pl.ds(owner * slab_rows, slab_rows)]
            return value * factor

        for distance in range(1, n_grp):
            put(box.at[distance], summed(lax.rem(group + distance, n_grp)))
            sends[distance - n_grp].start()
        if mine is None:
            put(box.at[0], summed(group))
            sends[0].start()
        else:
            mine[...] = summed(group)

    to_spectrum_and_back(trials.at[0], own)

    @pl.when(even)
    def _():
        send_out(own, False, outbox, near, out)

    @pl.when(jnp.logical_not(even))
    def _():
        store_total(own)

    own_copy.wait()

    @pl.when(even)
    def _():
        trial_copy.wait_recv()

    @pl.when(jnp.logical_not(even))
    def _():
        for copy in swap:
            copy.wait_recv()

    middle = pool.at[odd_index]
    to_spectrum_and_back(trials.at[1 - odd_index], middle)

    @pl.when(even)
    def _():
        store_total(middle)
        for copy in swap:
            copy.wait_recv()

    @pl.when(jnp.logical_not(even))
    def _():
        send_out(middle, True, outbox, near, out)
        total[...] = jnp.zeros_like(total)
        trial_copy.wait_recv()

    last = pool.at[1 - odd_index]
    to_spectrum_and_back(trials.at[1], last)
    send_out(last, True, far_outbox, far, None)

    result = out[...]
    for distance in range(1, n_grp):
        near[distance - 1].wait_recv()
        result = result + inbox[distance, 0:slab_rows].astype(f32)
    for distance in range(n_grp):
        far[distance].wait_recv()
        result = result + far_inbox[distance, 0:slab_rows].astype(f32)
    out[...] = result
    for copy in swap + near + far + [trial_copy]:
        copy.wait_send()


def local(n_orb, n_grp, targets, partners):
    copies = partners.shape[0]
    rows = X * ROWS_Y
    slab_rows = rows // n_grp
    padded = -(-slab_rows // 16) * 16
    factor = -1.0 / math.sqrt(STEPS * n_grp * copies)
    constants = tables(copies)
    vmem = pl.BlockSpec(memory_space=pltpu.VMEM)
    box = pltpu.VMEM((n_grp, padded, LANES), bf16)
    dma = pltpu.SemaphoreType.DMA
    result = pl.pallas_call(
        functools.partial(body, n_orb, n_grp, factor),
        out_shape=jax.ShapeDtypeStruct((slab_rows, LANES), f32),
        in_specs=[vmem] * 7,
        out_specs=vmem,
        scratch_shapes=[
            pltpu.VMEM((2, rows, LANES), bf16),
            pltpu.VMEM((3, copies, rows, LANES), bf16),
            pltpu.VMEM((X, ROWS_Y, FOLD * LANES), f32),
            pltpu.VMEM((X_BLOCKS, GROUPS, BLOCK_ROWS, LANES), bf16),
            pltpu.VMEM((rows, LANES), f32),
            box, box, box, box,
            dma, dma((2, copies)), dma((2,)),
            dma((n_grp,)), dma((n_grp,)), dma((n_grp,)), dma((n_grp,)),
        ],
        compiler_params=pltpu.CompilerParams(
            collective_id=0, has_side_effects=True, vmem_limit_bytes=32 * 1024 * 1024
        ),
    )(
        lax.optimization_barrier(targets.astype(f32)).reshape(rows, LANES),
        partners.reshape(copies, rows, LANES),
        *[jnp.asarray(table) for table in constants],
    )
    return result.reshape(1, slab_rows * LANES)


def solution(mesh):
    in_specs = (P("orb", None), P(("orb", "grp"), None))
    out_specs = P("orb", "grp")
    return jax.shard_map(
        functools.partial(local, mesh.shape["orb"], mesh.shape["grp"]),
        mesh=mesh, in_specs=in_specs, out_specs=out_specs, check_vma=False,
    )
```
